32 devices in a mesh: groups: 2 (over x), dp: 8 (over z, y), own: 2 (over core).
Axes of the slice: x: 2, y: 2, z: 4, core: 2. Of those that a mesh axis runs over, the one named last changes fastest.
Arguments:
- acts: bfloat16 [2048, 8192], P(('groups', 'dp')), parts along dimension 0, may hold values from -6 to 6
- grad_out: bfloat16 [2048, 8192], P(('groups', 'dp')), parts along dimension 0, may hold values from -6 to 6
- weight_blocks: bfloat16 [1664, 4096], P(('dp', 'own')), may hold values from -0.21875 to 0.21875
- block_rows: int32 [1664], replicated, may hold values from 0 to 127, as said below
- block_cols: int32 [1664], replicated, may hold values from 0 to 127, as said below
Outputs:
- grad_blocks: bfloat16 [3328, 4096], P(('groups', 'dp', 'own')), parts along dimension 0
- grad_acts: bfloat16 [2048, 8192], P(('groups', 'dp'), 'own'), parts along dimension 0
The draws below stay inside these ranges and needn't reach their ends.
There are 2 independent parts, one for each index of `groups`. The reference program is written for one: setup_inputs(seed, part) draws one part's arguments, and reference() takes and returns one part's arrays. A program takes and returns all parts, laid end to end along the dimension named above; an argument that names none is the same for every part. Nothing has to cross between parts.
Inputs may be any that keep to these rules, and one draw needn't show every extreme that they name: `block_rows`: together with block_cols at the same index it names one block of the 128 x 8192/64 grid of blocks; no block is named twice; block (0, 0) and the last block of the grid are always named. `block_cols`: see block_rows.
All inputs are finite; a program needn't handle non-finite values.
Results may differ from the reference program's by a relative error of at most 0.001.
Values may be sent and summed in bfloat16 or wider, within the bound.
A program may use at most 128 MiB of HBM per device.

```python
import math
import jax
import jax.numpy as jnp
from jax import lax

D = 8192
BLOCK = 64
NBLK = 1664
TOKENS = 1024


def pattern_ids(key):
    grid_total = (D // BLOCK) ** 2
    inner = jax.random.permutation(key, grid_total - 2)[:NBLK - 2] + 1
    chosen = jnp.concatenate([jnp.array([0, grid_total - 1], jnp.int32), inner.astype(jnp.int32)])
    order_key = jax.random.fold_in(key, 77)
    return chosen[jax.random.permutation(order_key, NBLK)].astype(jnp.int32)


def draw_block_rows(key, part):
    chosen = pattern_ids(key)
    return (chosen // (D // BLOCK)).astype(jnp.int32)


def draw_block_cols(key, part):
    chosen = pattern_ids(key)
    return (chosen % (D // BLOCK)).astype(jnp.int32)


def block_levels(rng, dims, cuts, low, largest):
    def one(axis_at, parts):
        draws = jax.random.uniform(jax.random.fold_in(jax.random.fold_in(rng, 6), axis_at), (parts,), jnp.float32, low / len(cuts), largest / len(cuts))
        return jnp.repeat(jnp.exp(draws), dims[axis_at] // parts).reshape((-1,) + (1,) * (len(dims) - axis_at - 1))

    level = one(*cuts[0])
    for cut in cuts[1:]:
        level = level * one(*cut)
    return level


def noise(own_key, shape, spread, limit, split=(), kind=jnp.bfloat16):
    result = jax.random.normal(own_key, shape, jnp.float32) * spread
    if len(split) > 0:
        result = block_levels(own_key, shape, split, -0.22, 0.18) * result
    return jnp.clip(result, min=-limit, max=limit).astype(kind)


def setup_inputs(seed: int = 0, part: int = 0) -> dict:
    splits = jax.random.split(jax.random.key(seed), 6)
    part_splits = jax.random.split(jax.random.fold_in(splits[5], part), 6)
    acts = noise(part_splits[0], (TOKENS, D), 1.0, 6.0, ((0, 8),))
    grad_out = noise(part_splits[1], (TOKENS, D), 1.0, 6.0, ((0, 8),))
    weight_blocks = noise(splits[2], (NBLK, BLOCK * BLOCK), (NBLK * BLOCK * BLOCK // D) ** -0.5, 0.21875, ((0, 16),))
    block_rows = draw_block_rows(jax.random.fold_in(splits[5], 71), part)
    block_cols = draw_block_cols(jax.random.fold_in(splits[5], 71), part)
    return {"acts": acts, "grad_out": grad_out, "weight_blocks": weight_blocks, "block_rows": block_rows, "block_cols": block_cols}


def reference(acts, grad_out, weight_blocks, block_rows, block_cols):
    tok_rows = acts.shape[0]
    row_blocks = D // BLOCK
    acts_three = acts.reshape(tok_rows, row_blocks, BLOCK)
    grad_three = grad_out.reshape(tok_rows, row_blocks, BLOCK)
    rows_grouped = block_rows.reshape(-1, 64)
    cols_grouped = block_cols.reshape(-1, 64)
    weights_grouped = weight_blocks.reshape(-1, 64, BLOCK, BLOCK)

    def block_grad(pair):
        rows_here, cols_here = pair
        left = acts_three[:, rows_here].astype(jnp.float32)
        right = grad_three[:, cols_here].astype(jnp.float32)
        return jnp.einsum('tbi,tbj->bij', left, right).reshape(64, BLOCK * BLOCK)
    summed = lax.map(block_grad, (rows_grouped, cols_grouped)).reshape(NBLK, BLOCK * BLOCK)
    grad_blocks = (summed * (1.0 / math.sqrt(TOKENS))).astype(jnp.bfloat16)

    def add_group(totals, triple):
        rows_here, cols_here, weights_here = triple
        right = grad_three[:, cols_here].astype(jnp.float32)
        contrib = jnp.einsum('tbj,bij->tbi', right, weights_here.astype(jnp.float32))
        return (totals.at[:, rows_here].add(contrib), None)
    start_totals = jnp.zeros((tok_rows, row_blocks, BLOCK), jnp.float32)
    totals, unused = lax.scan(add_group, start_totals, (rows_grouped, cols_grouped, weights_grouped))
    grad_acts = totals.reshape(tok_rows, D).astype(jnp.bfloat16)
    return (grad_blocks, grad_acts)
```

```python
import functools
import math

import jax
import jax.numpy as jnp
from jax import lax
from jax.experimental import pallas as pl
from jax.experimental.pallas import tpu as pltpu
from jax.sharding import PartitionSpec as P

BLOCK = 64
LANES = 2 * BLOCK
MIB = 1024 * 1024


def block_grad_kernel(scale, rows_ref, cols_ref, a0, a1, g0, g1, out_ref):
    pairs = out_ref.shape[0]
    start = pl.program_id(0) * pairs
    left_half = lax.broadcasted_iota(jnp.int32, (BLOCK, LANES), 1) < BLOCK

    def features(ref, other, at):
        rows = pl.ds(pl.multiple_of(at * BLOCK, BLOCK), BLOCK)
        return jnp.concatenate([ref[rows, :], other[rows, :]], axis=1)

    def one_pair(p, carry):
        b = 2 * (start + p)
        lhs = jnp.concatenate([features(a0, a1, rows_ref[b + k]) for k in range(2)], axis=0)
        rhs = jnp.concatenate([features(g0, g1, cols_ref[b + k]) for k in range(2)], axis=0)
        prod = lax.dot_general(
            lhs, rhs, (((1,), (1,)), ((), ())), preferred_element_type=jnp.float32
        )
        out_ref[p] = jnp.where(left_half, prod[:BLOCK], prod[BLOCK:]) * scale
        return carry

    lax.fori_loop(0, pairs, one_pair, 0, unroll=4)


def block_grads(rows, cols, a0, a1, g0, g1, scale, steps):
    pairs = rows.shape[0] // 2
    whole = pl.BlockSpec(a0.shape, lambda i, *_: (0, 0))
    return pl.pallas_call(
        functools.partial(block_grad_kernel, scale),
        out_shape=jax.ShapeDtypeStruct((pairs, BLOCK, LANES), jnp.float32),
        grid_spec=pltpu.PrefetchScalarGridSpec(
            num_scalar_prefetch=2,
            grid=(steps,),
            in_specs=[whole] * 4,
            out_specs=pl.BlockSpec((pairs // steps, BLOCK, LANES), lambda i, *_: (i, 0, 0)),
        ),
        compiler_params=pltpu.CompilerParams(vmem_limit_bytes=48 * MIB),
        cost_estimate=pl.CostEstimate(
            flops=pairs * 2 * LANES * LANES * 512, bytes_accessed=16 * MIB, transcendentals=0
        ),
        name="block_grads",
    )(rows, cols, a0, a1, g0, g1)


def input_grad_kernel(rows_ref, cols_ref, w_ref, g_ref, out_ref):
    pairs = w_ref.shape[0]
    start = pl.program_id(0) * pairs
    lane = lax.broadcasted_iota(jnp.int32, (BLOCK, LANES), 1)
    first = (lane < BLOCK).astype(jnp.float32).astype(jnp.bfloat16)
    second = (lane >= BLOCK).astype(jnp.float32).astype(jnp.bfloat16)

    @pl.when(pl.program_id(0) == 0)
    def _():
        out_ref[...] = jnp.zeros_like(out_ref)

    def span(at):
        return pl.ds(pl.multiple_of(at * BLOCK, BLOCK), BLOCK)

    def one_pair(p, carry):
        b = 2 * (start + p)
        w = w_ref[p]
        lhs = jnp.concatenate([w * first, w * second], axis=0)
        rhs = jnp.concatenate([g_ref[span(cols_ref[b + k]), :] for k in range(2)], axis=0)
        prod = jnp.dot(lhs, rhs, preferred_element_type=jnp.float32)
        for k in range(2):
            out_ref[span(rows_ref[b + k]), :] += prod[k * BLOCK : (k + 1) * BLOCK]
        return carry

    lax.fori_loop(0, pairs, one_pair, 0, unroll=4)


def input_grad(rows, cols, weights, g, steps):
    pairs = weights.shape[0]
    return pl.pallas_call(
        input_grad_kernel,
        out_shape=jax.ShapeDtypeStruct(g.shape, jnp.float32),
        grid_spec=pltpu.PrefetchScalarGridSpec(
            num_scalar_prefetch=2,
            grid=(steps,),
            in_specs=[
                pl.BlockSpec((pairs // steps, BLOCK, LANES), lambda i, *_: (i, 0, 0)),
                pl.BlockSpec(g.shape, lambda i, *_: (0, 0)),
            ],
            out_specs=pl.BlockSpec(g.shape, lambda i, *_: (0, 0)),
        ),
        compiler_params=pltpu.CompilerParams(vmem_limit_bytes=48 * MIB),
        cost_estimate=pl.CostEstimate(
            flops=pairs * 2 * LANES * LANES * 1024, bytes_accessed=13 * MIB, transcendentals=0
        ),
        name="input_grad",
    )(rows, cols, weights, g)


def per_device(acts, grad_out, weight_blocks, block_rows, block_cols):
    tok_rows, width = acts.shape
    n_data = lax.axis_size("dp")
    data_index = lax.axis_index("dp")
    own_index = lax.axis_index("own")
    local_blocks = weight_blocks.shape[0]
    scale = 1.0 / math.sqrt(tok_rows * n_data)

    w_pairs = (
        weight_blocks.reshape(local_blocks // 2, 2, BLOCK, BLOCK)
        .transpose(0, 2, 1, 3)
        .reshape(local_blocks // 2, BLOCK, LANES)
    )
    all_weights = lax.all_gather(w_pairs, "dp", axis=0, tiled=True)

    half = width // 2
    both = jnp.stack([acts, grad_out])
    both_half = lax.dynamic_slice_in_dim(both, own_index * half, half, axis=2)
    mine_t = both.transpose(0, 2, 1)
    half_t = both_half.transpose(0, 2, 1)
    swap = [(d, d ^ 1) for d in range(n_data)]
    came = lax.ppermute(half_t, "dp", swap)
    pair_t = lax.all_gather(came, "own", axis=1, tiled=True)

    by_owner_rows = block_rows.reshape(n_data // 2, 2, 2, local_blocks)
    by_owner_cols = block_cols.reshape(n_data // 2, 2, 2, local_blocks)
    half_rows = by_owner_rows[:, :, own_index]
    half_cols = by_owner_cols[:, :, own_index]
    sub_rows = half_rows[:, data_index % 2].reshape(-1)
    sub_cols = half_cols[:, data_index % 2].reshape(-1)

    partial = block_grads(
        sub_rows, sub_cols, mine_t[0], pair_t[0], mine_t[1], pair_t[1], scale, 4
    )
    later_rows, partial = lax.optimization_barrier((half_rows.reshape(-1), partial))
    groups = [list(range(k, n_data, 2)) for k in range(2)]
    summed = lax.psum_scatter(
        partial, "dp", scatter_dimension=0, axis_index_groups=groups, tiled=True
    )
    grad_blocks = (
        summed.astype(jnp.bfloat16)
        .reshape(local_blocks // 2, BLOCK, 2, BLOCK)
        .transpose(0, 2, 1, 3)
        .reshape(local_blocks, BLOCK * BLOCK)
    )

    total_t = input_grad(later_rows, half_cols.reshape(-1), all_weights, mine_t[1], 8)
    ga_t = lax.psum_scatter(total_t, "own", scatter_dimension=0, tiled=True)
    grad_acts = ga_t.astype(jnp.bfloat16).T
    return (grad_blocks, grad_acts)


def solution(mesh):
    in_specs = (
        P(("groups", "dp"), None),
        P(("groups", "dp"), None),
        P(("dp", "own"), None),
        P(),
        P(),
    )
    out_specs = (P(("groups", "dp", "own"), None), P(("groups", "dp"), "own"))
    return jax.shard_map(
        per_device, mesh=mesh, in_specs=in_specs, out_specs=out_specs, check_vma=False
    )
```

```python
import functools
import math

import jax
import jax.numpy as jnp
from jax import lax
from jax.experimental import pallas as pl
from jax.experimental.pallas import tpu as pltpu
from jax.sharding import PartitionSpec as P

BLOCK = 64
LANES = 2 * BLOCK
MIB = 1024 * 1024


LEVELS = 32767.0
SMALLEST = 1e-33
CHUNKS = 4
MESH = pl.DeviceIdType.MESH


def block_grad_kernel(
    scale,
    owners,
    rows_ref,
    cols_ref,
    a0,
    g0,
    out_ref,
    a1,
    g1,
    sent,
    sent_unit,
    came,
    came_unit,
    kept,
    over_sems,
    side_sems,
    word_sems,
    unit_sems,
):
    dp, own = lax.axis_index("dp"), lax.axis_index("own")
    n_data = 2 * owners
    pair = dp + 1 - 2 * lax.rem(dp, 2)
    each = out_ref.shape[0]
    half = a0.shape[0] // 2
    part = half // CHUNKS
    left_half = lax.broadcasted_iota(jnp.int32, (BLOCK, LANES), 1) < BLOCK

    barrier = pltpu.get_barrier_semaphore()
    pl.semaphore_signal(barrier, inc=1, device_id={"dp": pair}, device_id_type=MESH)
    pl.semaphore_signal(barrier, inc=1, device_id={"own": 1 - own}, device_id_type=MESH)
    for k in range(1, owners):
        pl.semaphore_signal(
            barrier,
            inc=1,
            device_id={"dp": lax.rem(dp + 2 * k, n_data)},
            device_id_type=MESH,
        )
    pl.semaphore_wait(barrier, owners + 1)

    def over(which, c):
        rows = pl.ds(own * half + c * part, part)
        return pltpu.make_async_remote_copy(
            src_ref=(a0, g0)[which].at[rows],
            dst_ref=(a1, g1)[which].at[rows],
            send_sem=over_sems.at[0, which, c],
            recv_sem=over_sems.at[1, which, c],
            device_id={"dp": pair},
            device_id_type=MESH,
        )

    def side(which, c):
        rows = pl.ds(own * half + c * part, part)
        target = (a1, g1)[which].at[rows]
        return pltpu.make_async_remote_copy(
            src_ref=target,
            dst_ref=target,
            send_sem=side_sems.at[0, which, c],
            recv_sem=side_sems.at[1, which, c],
            device_id={"own": 1 - own},
            device_id_type=MESH,
        )

    order = [(which, c) for c in range(CHUNKS) for which in range(2)]
    for which, c in order:
        over(which, c).start()
    for which, c in order:
        over(which, c).wait_recv()
        side(which, c).start()
    for which, c in order:
        side(which, c).wait_recv()

    def features(ref, other, at):
        return jnp.concatenate([ref[at], other[at]], axis=1)

    def pair_sum(p):
        b = 2 * p
        lhs = jnp.concatenate([features(a0, a1, rows_ref[b + k]) for k in range(2)], axis=0)
        rhs = jnp.concatenate([features(g0, g1, cols_ref[b + k]) for k in range(2)], axis=0)
        prod = lax.dot_general(
            lhs, rhs, (((1,), (1,)), ((), ())), preferred_element_type=jnp.float32
        )
        return jnp.where(left_half, prod[:BLOCK], prod[BLOCK:]) * scale

    def words(k):
        return pltpu.make_async_remote_copy(
            src_ref=sent.at[k - 1],
            dst_ref=came.at[k - 1],
            send_sem=word_sems.at[0, k - 1],
            recv_sem=word_sems.at[1, k - 1],
            device_id={"dp": lax.rem(dp + 2 * k, n_data)},
            device_id_type=MESH,
        )

    def steps(k):
        return pltpu.make_async_remote_copy(
            src_ref=sent_unit.at[k - 1],
            dst_ref=came_unit.at[k - 1],
            send_sem=unit_sems.at[0, k - 1],
            recv_sem=unit_sems.at[1, k - 1],
            device_id={"dp": lax.rem(dp + 2 * k, n_data)},
            device_id_type=MESH,
        )

    def send_one(k, carry):
        def pack(p, inner):
            total = pair_sum(k * each + p)
            peak = jnp.maximum(jnp.max(jnp.abs(total), axis=0, keepdims=True), SMALLEST)
            levels = jnp.floor(total * (LEVELS / peak) + 0.5).astype(jnp.int32)
            levels = jnp.clip(levels, -32767, 32767)
            sent[k - 1, p] = levels[: BLOCK // 2] * 65536 + levels[BLOCK // 2 :]
            sent_unit[k - 1, pl.ds(p, 1), :] = peak * (1.0 / LEVELS)
            return inner

        lax.fori_loop(0, each, pack, 0, unroll=4)
        words(k).start()
        steps(k).start()
        return carry

    lax.fori_loop(1, owners, send_one, 0)

    def keep(p, carry):
        kept[p] = pair_sum(p)
        return carry

    lax.fori_loop(0, each, keep, 0, unroll=4)

    def wait_one(k, carry):
        words(k).wait_recv()
        steps(k).wait_recv()
        return carry

    lax.fori_loop(1, owners, wait_one, 0)

    def add(p, carry):
        top = kept[p, : BLOCK // 2]
        low = kept[p, BLOCK // 2 :]
        for k in range(owners - 1):
            word = came[k, p]
            unit = came_unit[k, pl.ds(p, 1), :]
            low_levels = lax.shift_right_arithmetic(lax.shift_left(word, 16), 16)
            top_levels = lax.shift_right_arithmetic(word - low_levels, 16)
            top = top + top_levels.astype(jnp.float32) * unit
            low = low + low_levels.astype(jnp.float32) * unit
        out_ref[p] = jnp.concatenate([top, low], axis=0).astype(jnp.bfloat16)
        return carry

    lax.fori_loop(0, each, add, 0, unroll=2)

    for which, c in order:
        over(which, c).wait_send()
        side(which, c).wait_send()

    def sent_one(k, carry):
        words(k).wait_send()
        steps(k).wait_send()
        return carry

    lax.fori_loop(1, owners, sent_one, 0)


def block_grads(rows, cols, a0, g0, scale, owners):
    a0, g0 = (x.reshape(-1, BLOCK, x.shape[1]) for x in (a0, g0))
    each = rows.shape[0] // 2 // owners
    padded = -(-each // 8) * 8
    smem = pl.BlockSpec(memory_space=pltpu.SMEM)
    vmem = pl.BlockSpec(memory_space=pltpu.VMEM)
    return pl.pallas_call(
        functools.partial(block_grad_kernel, scale, owners),
        out_shape=jax.ShapeDtypeStruct((each, BLOCK, LANES), jnp.bfloat16),
        in_specs=[smem, smem, vmem, vmem],
        out_specs=vmem,
        scratch_shapes=[
            pltpu.VMEM(a0.shape, a0.dtype),
            pltpu.VMEM(g0.shape, g0.dtype),
            pltpu.VMEM((owners - 1, each, BLOCK // 2, LANES), jnp.int32),
            pltpu.VMEM((owners - 1, padded, LANES), jnp.float32),
            pltpu.VMEM((owners - 1, each, BLOCK // 2, LANES), jnp.int32),
            pltpu.VMEM((owners - 1, padded, LANES), jnp.float32),
            pltpu.VMEM((each, BLOCK, LANES), jnp.float32),
            pltpu.SemaphoreType.DMA((2, 2, CHUNKS)),
            pltpu.SemaphoreType.DMA((2, 2, CHUNKS)),
            pltpu.SemaphoreType.DMA((2, owners - 1)),
            pltpu.SemaphoreType.DMA((2, owners - 1)),
        ],
        compiler_params=pltpu.CompilerParams(
            vmem_limit_bytes=48 * MIB, collective_id=0, has_side_effects=True
        ),
        cost_estimate=pl.CostEstimate(
            flops=100_000_000_000, bytes_accessed=16 * MIB, transcendentals=0
        ),
        name="block_grads",
    )(rows, cols, a0, g0)


def input_grad_kernel(rows_ref, cols_ref, w_ref, g_ref, out_ref):
    pairs = w_ref.shape[0]
    start = pl.program_id(0) * pairs
    lane = lax.broadcasted_iota(jnp.int32, (BLOCK, LANES), 1)
    first = (lane < BLOCK).astype(jnp.float32).astype(jnp.bfloat16)
    second = (lane >= BLOCK).astype(jnp.float32).astype(jnp.bfloat16)

    @pl.when(pl.program_id(0) == 0)
    def _():
        out_ref[...] = jnp.zeros_like(out_ref)

    def span(at):
        return pl.ds(pl.multiple_of(at * BLOCK, BLOCK), BLOCK)

    def one_pair(p, carry):
        b = 2 * (start + p)
        w = w_ref[p]
        lhs = jnp.concatenate([w * first, w * second], axis=0)
        rhs = jnp.concatenate([g_ref[span(cols_ref[b + k]), :] for k in range(2)], axis=0)
        prod = jnp.dot(lhs, rhs, preferred_element_type=jnp.float32)
        for k in range(2):
            out_ref[span(rows_ref[b + k]), :] += prod[k * BLOCK : (k + 1) * BLOCK]
        return carry

    lax.fori_loop(0, pairs, one_pair, 0, unroll=4)


def input_grad(rows, cols, weights, g, steps):
    pairs = weights.shape[0]
    return pl.pallas_call(
        input_grad_kernel,
        out_shape=jax.ShapeDtypeStruct(g.shape, jnp.float32),
        grid_spec=pltpu.PrefetchScalarGridSpec(
            num_scalar_prefetch=2,
            grid=(steps,),
            in_specs=[
                pl.BlockSpec((pairs // steps, BLOCK, LANES), lambda i, *_: (i, 0, 0)),
                pl.BlockSpec(g.shape, lambda i, *_: (0, 0)),
            ],
            out_specs=pl.BlockSpec(g.shape, lambda i, *_: (0, 0)),
        ),
        compiler_params=pltpu.CompilerParams(vmem_limit_bytes=48 * MIB),
        cost_estimate=pl.CostEstimate(
            flops=pairs * 2 * LANES * LANES * 1024, bytes_accessed=13 * MIB, transcendentals=0
        ),
        name="input_grad",
    )(rows, cols, weights, g)


def per_device(acts, grad_out, weight_blocks, block_rows, block_cols):
    tok_rows, width = acts.shape
    n_data = lax.axis_size("dp")
    data_index = lax.axis_index("dp")
    own_index = lax.axis_index("own")
    local_blocks = weight_blocks.shape[0]
    scale = 1.0 / math.sqrt(tok_rows * n_data)

    w_pairs = (
        weight_blocks.reshape(local_blocks // 2, 2, BLOCK, BLOCK)
        .transpose(0, 2, 1, 3)
        .reshape(local_blocks // 2, BLOCK, LANES)
    )
    all_weights = lax.all_gather(w_pairs, "dp", axis=0, tiled=True)
    acts_t, grad_t = acts.T, grad_out.T
    acts_t, w_pairs = lax.optimization_barrier((acts_t, w_pairs))

    owners = n_data // 2
    by_owner_rows = block_rows.reshape(owners, 2, 2, local_blocks)
    by_owner_cols = block_cols.reshape(owners, 2, 2, local_blocks)
    half_rows = by_owner_rows[:, :, own_index]
    half_cols = by_owner_cols[:, :, own_index]

    def from_here(table):
        ours = jnp.roll(table[:, data_index % 2], -(data_index // 2), axis=0)
        return ours.reshape(-1)

    sums = block_grads(
        from_here(half_rows), from_here(half_cols), acts_t, grad_t, scale, owners
    )
    later_rows, sums = lax.optimization_barrier((half_rows.reshape(-1), sums))
    grad_blocks = (
        sums.reshape(local_blocks // 2, BLOCK, 2, BLOCK)
        .transpose(0, 2, 1, 3)
        .reshape(local_blocks, BLOCK * BLOCK)
    )
    total_t = input_grad(later_rows, half_cols.reshape(-1), all_weights, grad_t, 8)
    ga_t = lax.psum_scatter(total_t, "own", scatter_dimension=0, tiled=True)
    grad_acts = ga_t.astype(jnp.bfloat16).T
    return (grad_blocks, grad_acts)


def solution(mesh):
    in_specs = (
        P(("groups", "dp"), None),
        P(("groups", "dp"), None),
        P(("dp", "own"), None),
        P(),
        P(),
    )
    out_specs = (P(("groups", "dp", "own"), None), P(("groups", "dp"), "own"))
    return jax.shard_map(
        per_device, mesh=mesh, in_specs=in_specs, out_specs=out_specs, check_vma=False
    )
```

```python
import functools
import math

import jax
import jax.numpy as jnp
from jax import lax
from jax.experimental import pallas as pl
from jax.experimental.pallas import tpu as pltpu
from jax.sharding import PartitionSpec as P

BLOCK = 64
LANES = 2 * BLOCK
MIB = 1024 * 1024


LEVELS = 32767.0
SMALLEST = 1e-33
CHUNKS = 4
JOIN_CHUNKS = 4
MESH = pl.DeviceIdType.MESH


def block_grad_kernel(
    scale,
    owners,
    rows_ref,
    cols_ref,
    a0,
    g0,
    out_ref,
    a1,
    g1,
    sent,
    sent_unit,
    came,
    came_unit,
    kept,
    over_sems,
    side_sems,
    word_sems,
    unit_sems,
):
    dp, own = lax.axis_index("dp"), lax.axis_index("own")
    n_data = 2 * owners
    pair = dp + 1 - 2 * lax.rem(dp, 2)
    each = out_ref.shape[0]
    half = a0.shape[0] // 2
    part = half // CHUNKS
    left_half = lax.broadcasted_iota(jnp.int32, (BLOCK, LANES), 1) < BLOCK

    barrier = pltpu.get_barrier_semaphore()
    pl.semaphore_signal(barrier, inc=1, device_id={"dp": pair}, device_id_type=MESH)
    pl.semaphore_signal(barrier, inc=1, device_id={"own": 1 - own}, device_id_type=MESH)
    for k in range(1, owners):
        pl.semaphore_signal(
            barrier,
            inc=1,
            device_id={"dp": lax.rem(dp + 2 * k, n_data)},
            device_id_type=MESH,
        )
    pl.semaphore_wait(barrier, owners + 1)

    def over(which, c):
        rows = pl.ds(own * half + c * part, part)
        return pltpu.make_async_remote_copy(
            src_ref=(a0, g0)[which].at[rows],
            dst_ref=(a1, g1)[which].at[rows],
            send_sem=over_sems.at[0, which, c],
            recv_sem=over_sems.at[1, which, c],
            device_id={"dp": pair},
            device_id_type=MESH,
        )

    def side(which, c):
        rows = pl.ds(own * half + c * part, part)
        target = (a1, g1)[which].at[rows]
        return pltpu.make_async_remote_copy(
            src_ref=target,
            dst_ref=target,
            send_sem=side_sems.at[0, which, c],
            recv_sem=side_sems.at[1, which, c],
            device_id={"own": 1 - own},
            device_id_type=MESH,
        )

    order = [(which, c) for c in range(CHUNKS) for which in range(2)]
    for which, c in order:
        over(which, c).start()
    for which, c in order:
        over(which, c).wait_recv()
        side(which, c).start()
    for which, c in order:
        side(which, c).wait_recv()

    def features(ref, other, at):
        return jnp.concatenate([ref[at], other[at]], axis=1)

    def pair_sum(p):
        b = 2 * p
        lhs = jnp.concatenate([features(a0, a1, rows_ref[b + k]) for k in range(2)], axis=0)
        rhs = jnp.concatenate([features(g0, g1, cols_ref[b + k]) for k in range(2)], axis=0)
        prod = lax.dot_general(
            lhs, rhs, (((1,), (1,)), ((), ())), preferred_element_type=jnp.float32
        )
        return jnp.where(left_half, prod[:BLOCK], prod[BLOCK:]) * scale

    def words(k):
        return pltpu.make_async_remote_copy(
            src_ref=sent.at[k - 1],
            dst_ref=came.at[k - 1],
            send_sem=word_sems.at[0, k - 1],
            recv_sem=word_sems.at[1, k - 1],
            device_id={"dp": lax.rem(dp + 2 * k, n_data)},
            device_id_type=MESH,
        )

    def steps(k):
        return pltpu.make_async_remote_copy(
            src_ref=sent_unit.at[k - 1],
            dst_ref=came_unit.at[k - 1],
            send_sem=unit_sems.at[0, k - 1],
            recv_sem=unit_sems.at[1, k - 1],
            device_id={"dp": lax.rem(dp + 2 * k, n_data)},
            device_id_type=MESH,
        )

    def send_one(k, carry):
        def pack(p, inner):
            total = pair_sum(k * each + p)
            peak = jnp.maximum(jnp.max(jnp.abs(total), axis=0, keepdims=True), SMALLEST)
            levels = jnp.floor(total * (LEVELS / peak) + 0.5).astype(jnp.int32)
            levels = jnp.clip(levels, -32767, 32767)
            sent[k - 1, p] = levels[: BLOCK // 2] * 65536 + levels[BLOCK // 2 :]
            sent_unit[k - 1, pl.ds(p, 1), :] = peak * (1.0 / LEVELS)
            return inner

        lax.fori_loop(0, each, pack, 0, unroll=4)
        words(k).start()
        steps(k).start()
        return carry

    lax.fori_loop(1, owners, send_one, 0)

    def keep(p, carry):
        kept[p] = pair_sum(p)
        return carry

    lax.fori_loop(0, each, keep, 0, unroll=4)

    def wait_one(k, carry):
        words(k).wait_recv()
        steps(k).wait_recv()
        return carry

    lax.fori_loop(1, owners, wait_one, 0)

    def add(p, carry):
        top = kept[p, : BLOCK // 2]
        low = kept[p, BLOCK // 2 :]
        for k in range(owners - 1):
            word = came[k, p]
            unit = came_unit[k, pl.ds(p, 1), :]
            low_levels = lax.shift_right_arithmetic(lax.shift_left(word, 16), 16)
            top_levels = lax.shift_right_arithmetic(word - low_levels, 16)
            top = top + top_levels.astype(jnp.float32) * unit
            low = low + low_levels.astype(jnp.float32) * unit
        out_ref[p] = jnp.concatenate([top, low], axis=0).astype(jnp.bfloat16)
        return carry

    lax.fori_loop(0, each, add, 0, unroll=2)

    for which, c in order:
        over(which, c).wait_send()
        side(which, c).wait_send()

    def sent_one(k, carry):
        words(k).wait_send()
        steps(k).wait_send()
        return carry

    lax.fori_loop(1, owners, sent_one, 0)


def block_grads(rows, cols, a0, g0, scale, owners):
    a0, g0 = (x.reshape(-1, BLOCK, x.shape[1]) for x in (a0, g0))
    each = rows.shape[0] // 2 // owners
    padded = -(-each // 8) * 8
    smem = pl.BlockSpec(memory_space=pltpu.SMEM)
    vmem = pl.BlockSpec(memory_space=pltpu.VMEM)
    return pl.pallas_call(
        functools.partial(block_grad_kernel, scale, owners),
        out_shape=jax.ShapeDtypeStruct((each, BLOCK, LANES), jnp.bfloat16),
        in_specs=[smem, smem, vmem, vmem],
        out_specs=vmem,
        scratch_shapes=[
            pltpu.VMEM(a0.shape, a0.dtype),
            pltpu.VMEM(g0.shape, g0.dtype),
            pltpu.VMEM((owners - 1, each, BLOCK // 2, LANES), jnp.int32),
            pltpu.VMEM((owners - 1, padded, LANES), jnp.float32),
            pltpu.VMEM((owners - 1, each, BLOCK // 2, LANES), jnp.int32),
            pltpu.VMEM((owners - 1, padded, LANES), jnp.float32),
            pltpu.VMEM((each, BLOCK, LANES), jnp.float32),
            pltpu.SemaphoreType.DMA((2, 2, CHUNKS)),
            pltpu.SemaphoreType.DMA((2, 2, CHUNKS)),
            pltpu.SemaphoreType.DMA((2, owners - 1)),
            pltpu.SemaphoreType.DMA((2, owners - 1)),
        ],
        compiler_params=pltpu.CompilerParams(
            vmem_limit_bytes=48 * MIB, collective_id=0, has_side_effects=True
        ),
        cost_estimate=pl.CostEstimate(
            flops=100_000_000_000, bytes_accessed=16 * MIB, transcendentals=0
        ),
        name="block_grads",
    )(rows, cols, a0, g0)


def input_grad_kernel(rows_ref, cols_ref, w_ref, g_ref, out_ref):
    pairs = w_ref.shape[0]
    start = pl.program_id(0) * pairs
    lane = lax.broadcasted_iota(jnp.int32, (BLOCK, LANES), 1)
    first = (lane < BLOCK).astype(jnp.float32).astype(jnp.bfloat16)
    second = (lane >= BLOCK).astype(jnp.float32).astype(jnp.bfloat16)

    @pl.when(pl.program_id(0) == 0)
    def _():
        out_ref[...] = jnp.zeros_like(out_ref)

    def span(at):
        return pl.ds(pl.multiple_of(at * BLOCK, BLOCK), BLOCK)

    def one_pair(p, carry):
        b = 2 * (start + p)
        w = w_ref[p]
        lhs = jnp.concatenate([w * first, w * second], axis=0)
        rhs = jnp.concatenate([g_ref[span(cols_ref[b + k]), :] for k in range(2)], axis=0)
        prod = jnp.dot(lhs, rhs, preferred_element_type=jnp.float32)
        for k in range(2):
            out_ref[span(rows_ref[b + k]), :] += prod[k * BLOCK : (k + 1) * BLOCK]
        return carry

    lax.fori_loop(0, pairs, one_pair, 0, unroll=4)


def input_grad(rows, cols, weights, g, steps):
    pairs = weights.shape[0]
    return pl.pallas_call(
        input_grad_kernel,
        out_shape=jax.ShapeDtypeStruct(g.shape, jnp.float32),
        grid_spec=pltpu.PrefetchScalarGridSpec(
            num_scalar_prefetch=2,
            grid=(steps,),
            in_specs=[
                pl.BlockSpec((pairs // steps, BLOCK, LANES), lambda i, *_: (i, 0, 0)),
                pl.BlockSpec(g.shape, lambda i, *_: (0, 0)),
            ],
            out_specs=pl.BlockSpec(g.shape, lambda i, *_: (0, 0)),
        ),
        compiler_params=pltpu.CompilerParams(vmem_limit_bytes=48 * MIB),
        cost_estimate=pl.CostEstimate(
            flops=pairs * 2 * LANES * LANES * 1024, bytes_accessed=13 * MIB, transcendentals=0
        ),
        name="input_grad",
    )(rows, cols, weights, g)


def join_kernel(total_ref, out_ref, came, sems):
    own = lax.axis_index("own")
    barrier = pltpu.get_barrier_semaphore()
    pl.semaphore_signal(barrier, inc=1, device_id={"own": 1 - own}, device_id_type=MESH)
    pl.semaphore_wait(barrier, 1)
    half = came.shape[0]
    part = half // JOIN_CHUNKS

    def rows(which, c):
        return pl.ds(pl.multiple_of(which * half + c * part, part), part)

    def give(c):
        return pltpu.make_async_remote_copy(
            src_ref=total_ref.at[rows(1 - own, c), :],
            dst_ref=came.at[pl.ds(c * part, part), :],
            send_sem=sems.at[0, c],
            recv_sem=sems.at[1, c],
            device_id={"own": 1 - own},
            device_id_type=MESH,
        )

    for c in range(JOIN_CHUNKS):
        give(c).start()
    for c in range(JOIN_CHUNKS):
        give(c).wait_recv()
        both = total_ref[rows(own, c), :] + came[pl.ds(c * part, part), :]
        out_ref[:, pl.ds(c * part, part)] = both.T.astype(jnp.bfloat16)
    for c in range(JOIN_CHUNKS):
        give(c).wait_send()


def join_halves(total_t):
    width, tok_rows = total_t.shape
    vmem = pl.BlockSpec(memory_space=pltpu.VMEM)
    return pl.pallas_call(
        join_kernel,
        out_shape=jax.ShapeDtypeStruct((tok_rows, width // 2), jnp.bfloat16),
        in_specs=[vmem],
        out_specs=vmem,
        scratch_shapes=[
            pltpu.VMEM((width // 2, tok_rows), jnp.float32),
            pltpu.SemaphoreType.DMA((2, JOIN_CHUNKS)),
        ],
        compiler_params=pltpu.CompilerParams(
            vmem_limit_bytes=48 * MIB, collective_id=1, has_side_effects=True
        ),
        name="join_halves",
    )(total_t)


def per_device(acts, grad_out, weight_blocks, block_rows, block_cols):
    tok_rows, width = acts.shape
    n_data = lax.axis_size("dp")
    data_index = lax.axis_index("dp")
    own_index = lax.axis_index("own")
    local_blocks = weight_blocks.shape[0]
    scale = 1.0 / math.sqrt(tok_rows * n_data)

    w_pairs = (
        weight_blocks.reshape(local_blocks // 2, 2, BLOCK, BLOCK)
        .transpose(0, 2, 1, 3)
        .reshape(local_blocks // 2, BLOCK, LANES)
    )
    all_weights = lax.all_gather(w_pairs, "dp", axis=0, tiled=True)
    acts_t, grad_t = acts.T, grad_out.T
    acts_t, w_pairs = lax.optimization_barrier((acts_t, w_pairs))

    owners = n_data // 2
    by_owner_rows = block_rows.reshape(owners, 2, 2, local_blocks)
    by_owner_cols = block_cols.reshape(owners, 2, 2, local_blocks)
    half_rows = by_owner_rows[:, :, own_index]
    half_cols = by_owner_cols[:, :, own_index]

    def from_here(table):
        ours = jnp.roll(table[:, data_index % 2], -(data_index // 2), axis=0)
        return ours.reshape(-1)

    sums = block_grads(
        from_here(half_rows), from_here(half_cols), acts_t, grad_t, scale, owners
    )
    later_rows, sums = lax.optimization_barrier((half_rows.reshape(-1), sums))
    grad_blocks = (
        sums.reshape(local_blocks // 2, BLOCK, 2, BLOCK)
        .transpose(0, 2, 1, 3)
        .reshape(local_blocks, BLOCK * BLOCK)
    )
    total_t = input_grad(later_rows, half_cols.reshape(-1), all_weights, grad_t, 8)
    grad_acts = join_halves(total_t)
    return (grad_blocks, grad_acts)


def solution(mesh):
    in_specs = (
        P(("groups", "dp"), None),
        P(("groups", "dp"), None),
        P(("dp", "own"), None),
        P(),
        P(),
    )
    out_specs = (P(("groups", "dp", "own"), None), P(("groups", "dp"), "own"))
    return jax.shard_map(
        per_device, mesh=mesh, in_specs=in_specs, out_specs=out_specs, check_vma=False
    )
```

```python
import functools
import math

import jax
import jax.numpy as jnp
from jax import lax
from jax.experimental import pallas as pl
from jax.experimental.pallas import tpu as pltpu
from jax.sharding import PartitionSpec as P

BLOCK = 64
LANES = 2 * BLOCK
MIB = 1024 * 1024


LEVELS = 32767.0
SMALLEST = 1e-33
CHUNKS = 4
JOIN_CHUNKS = 4
MESH = pl.DeviceIdType.MESH


def exchange_kernel(a0, g0, a1, g1, over_sems, side_sems):
    dp, own = lax.axis_index("dp"), lax.axis_index("own")
    pair = dp + 1 - 2 * lax.rem(dp, 2)
    half = a0.shape[0] // 2
    part = half // CHUNKS

    barrier = pltpu.get_barrier_semaphore()
    pl.semaphore_signal(barrier, inc=1, device_id={"dp": pair}, device_id_type=MESH)
    pl.semaphore_signal(barrier, inc=1, device_id={"own": 1 - own}, device_id_type=MESH)
    pl.semaphore_wait(barrier, 2)

    def over(which, c):
        rows = pl.ds(own * half + c * part, part)
        return pltpu.make_async_remote_copy(
            src_ref=(a0, g0)[which].at[rows],
            dst_ref=(a1, g1)[which].at[rows],
            send_sem=over_sems.at[0, which, c],
            recv_sem=over_sems.at[1, which, c],
            device_id={"dp": pair},
            device_id_type=MESH,
        )

    def side(which, c):
        rows = pl.ds(own * half + c * part, part)
        target = (a1, g1)[which].at[rows]
        return pltpu.make_async_remote_copy(
            src_ref=target,
            dst_ref=target,
            send_sem=side_sems.at[0, which, c],
            recv_sem=side_sems.at[1, which, c],
            device_id={"own": 1 - own},
            device_id_type=MESH,
        )

    order = [(which, c) for c in range(CHUNKS) for which in range(2)]
    for which, c in order:
        over(which, c).start()
    for which, c in order:
        over(which, c).wait_recv()
        side(which, c).start()
    for which, c in order:
        side(which, c).wait_recv()
    for which, c in order:
        over(which, c).wait_send()
        side(which, c).wait_send()


def exchange(a0, g0):
    vmem = pl.BlockSpec(memory_space=pltpu.VMEM)
    return pl.pallas_call(
        exchange_kernel,
        out_shape=(
            jax.ShapeDtypeStruct(a0.shape, a0.dtype),
            jax.ShapeDtypeStruct(g0.shape, g0.dtype),
        ),
        in_specs=[vmem, vmem],
        out_specs=(vmem, vmem),
        scratch_shapes=[
            pltpu.SemaphoreType.DMA((2, 2, CHUNKS)),
            pltpu.SemaphoreType.DMA((2, 2, CHUNKS)),
        ],
        compiler_params=pltpu.CompilerParams(
            vmem_limit_bytes=48 * MIB, collective_id=2, has_side_effects=True
        ),
        name="exchange",
    )(a0, g0)


def block_grad_kernel(
    scale,
    owners,
    rows_ref,
    cols_ref,
    a0,
    g0,
    a1,
    g1,
    out_ref,
    sent,
    sent_unit,
    came,
    came_unit,
    kept,
    word_sems,
    unit_sems,
):
    dp = lax.axis_index("dp")
    n_data = 2 * owners
    each = out_ref.shape[0]
    left_half = lax.broadcasted_iota(jnp.int32, (BLOCK, LANES), 1) < BLOCK

    barrier = pltpu.get_barrier_semaphore()
    for k in range(1, owners):
        pl.semaphore_signal(
            barrier,
            inc=1,
            device_id={"dp": lax.rem(dp + 2 * k, n_data)},
            device_id_type=MESH,
        )
    pl.semaphore_wait(barrier, owners - 1)

    def features(ref, other, at):
        return jnp.concatenate([ref[at], other[at]], axis=1)

    def pair_sum(p):
        b = 2 * p
        lhs = jnp.concatenate([features(a0, a1, rows_ref[b + k]) for k in range(2)], axis=0)
        rhs = jnp.concatenate([features(g0, g1, cols_ref[b + k]) for k in range(2)], axis=0)
        prod = lax.dot_general(
            lhs, rhs, (((1,), (1,)), ((), ())), preferred_element_type=jnp.float32
        )
        return jnp.where(left_half, prod[:BLOCK], prod[BLOCK:]) * scale

    def words(k):
        return pltpu.make_async_remote_copy(
            src_ref=sent.at[k - 1],
            dst_ref=came.at[k - 1],
            send_sem=word_sems.at[0, k - 1],
            recv_sem=word_sems.at[1, k - 1],
            device_id={"dp": lax.rem(dp + 2 * k, n_data)},
            device_id_type=MESH,
        )

    def steps(k):
        return pltpu.make_async_remote_copy(
            src_ref=sent_unit.at[k - 1],
            dst_ref=came_unit.at[k - 1],
            send_sem=unit_sems.at[0, k - 1],
            recv_sem=unit_sems.at[1, k - 1],
            device_id={"dp": lax.rem(dp + 2 * k, n_data)},
            device_id_type=MESH,
        )

    def send_one(k, carry):
        def pack(p, inner):
            total = pair_sum(k * each + p)
            peak = jnp.maximum(jnp.max(jnp.abs(total), axis=0, keepdims=True), SMALLEST)
            levels = jnp.floor(total * (LEVELS / peak) + 0.5).astype(jnp.int32)
            levels = jnp.clip(levels, -32767, 32767)
            sent[k - 1, p] = levels[: BLOCK // 2] * 65536 + levels[BLOCK // 2 :]
            sent_unit[k - 1, pl.ds(p, 1), :] = peak * (1.0 / LEVELS)
            return inner

        lax.fori_loop(0, each, pack, 0, unroll=4)
        words(k).start()
        steps(k).start()
        return carry

    lax.fori_loop(1, owners, send_one, 0)

    def keep(p, carry):
        kept[p] = pair_sum(p)
        return carry

    lax.fori_loop(0, each, keep, 0, unroll=4)

    def wait_one(k, carry):
        words(k).wait_recv()
        steps(k).wait_recv()
        return carry

    lax.fori_loop(1, owners, wait_one, 0)

    def add(p, carry):
        top = kept[p, : BLOCK // 2]
        low = kept[p, BLOCK // 2 :]
        for k in range(owners - 1):
            word = came[k, p]
            unit = came_unit[k, pl.ds(p, 1), :]
            low_levels = lax.shift_right_arithmetic(lax.shift_left(word, 16), 16)
            top_levels = lax.shift_right_arithmetic(word - low_levels, 16)
            top = top + top_levels.astype(jnp.float32) * unit
            low = low + low_levels.astype(jnp.float32) * unit
        out_ref[p] = jnp.concatenate([top, low], axis=0).astype(jnp.bfloat16)
        return carry

    lax.fori_loop(0, each, add, 0, unroll=2)

    def sent_one(k, carry):
        words(k).wait_send()
        steps(k).wait_send()
        return carry

    lax.fori_loop(1, owners, sent_one, 0)


def block_grads(rows, cols, a0, g0, a1, g1, scale, owners):
    each = rows.shape[0] // 2 // owners
    padded = -(-each // 8) * 8
    smem = pl.BlockSpec(memory_space=pltpu.SMEM)
    vmem = pl.BlockSpec(memory_space=pltpu.VMEM)
    return pl.pallas_call(
        functools.partial(block_grad_kernel, scale, owners),
        out_shape=jax.ShapeDtypeStruct((each, BLOCK, LANES), jnp.bfloat16),
        in_specs=[smem, smem, vmem, vmem, vmem, vmem],
        out_specs=vmem,
        scratch_shapes=[
            pltpu.VMEM((owners - 1, each, BLOCK // 2, LANES), jnp.int32),
            pltpu.VMEM((owners - 1, padded, LANES), jnp.float32),
            pltpu.VMEM((owners - 1, each, BLOCK // 2, LANES), jnp.int32),
            pltpu.VMEM((owners - 1, padded, LANES), jnp.float32),
            pltpu.VMEM((each, BLOCK, LANES), jnp.float32),
            pltpu.SemaphoreType.DMA((2, owners - 1)),
            pltpu.SemaphoreType.DMA((2, owners - 1)),
        ],
        compiler_params=pltpu.CompilerParams(
            vmem_limit_bytes=48 * MIB, collective_id=0, has_side_effects=True
        ),
        cost_estimate=pl.CostEstimate(
            flops=100_000_000_000, bytes_accessed=16 * MIB, transcendentals=0
        ),
        name="block_grads",
    )(rows, cols, a0, g0, a1, g1)


def input_grad_kernel(rows_ref, cols_ref, w_ref, g_ref, out_ref):
    pairs = w_ref.shape[1]
    start = pl.program_id(0) * pairs
    lane = lax.broadcasted_iota(jnp.int32, (BLOCK, LANES), 1)
    first = (lane < BLOCK).astype(jnp.float32).astype(jnp.bfloat16)
    second = (lane >= BLOCK).astype(jnp.float32).astype(jnp.bfloat16)

    @pl.when(pl.program_id(0) == 0)
    def _():
        out_ref[...] = jnp.zeros_like(out_ref)

    def span(at):
        return pl.ds(pl.multiple_of(at * BLOCK, BLOCK), BLOCK)

    def one_pair(p, carry):
        b = 2 * (start + p)
        w = jnp.concatenate([w_ref[0, p], w_ref[1, p]], axis=0)
        lhs = jnp.concatenate([w * first, w * second], axis=0)
        rhs = jnp.concatenate([g_ref[span(cols_ref[b + k]), :] for k in range(2)], axis=0)
        prod = jnp.dot(lhs, rhs, preferred_element_type=jnp.float32)
        for k in range(2):
            out_ref[span(rows_ref[b + k]), :] += prod[k * BLOCK : (k + 1) * BLOCK]
        return carry

    lax.fori_loop(0, pairs, one_pair, 0, unroll=4)


def input_grad(rows, cols, weights, g, steps):
    pairs = weights.shape[1]
    return pl.pallas_call(
        input_grad_kernel,
        out_shape=jax.ShapeDtypeStruct(g.shape, jnp.float32),
        grid_spec=pltpu.PrefetchScalarGridSpec(
            num_scalar_prefetch=2,
            grid=(steps,),
            in_specs=[
                pl.BlockSpec(
                    (2, pairs // steps, BLOCK // 2, LANES), lambda i, *_: (0, i, 0, 0)
                ),
                pl.BlockSpec(g.shape, lambda i, *_: (0, 0)),
            ],
            out_specs=pl.BlockSpec(g.shape, lambda i, *_: (0, 0)),
        ),
        compiler_params=pltpu.CompilerParams(vmem_limit_bytes=48 * MIB),
        cost_estimate=pl.CostEstimate(
            flops=pairs * 2 * LANES * LANES * 1024, bytes_accessed=13 * MIB, transcendentals=0
        ),
        name="input_grad",
    )(rows, cols, weights, g)


def join_kernel(total_ref, out_ref, came, sems):
    own = lax.axis_index("own")
    barrier = pltpu.get_barrier_semaphore()
    pl.semaphore_signal(barrier, inc=1, device_id={"own": 1 - own}, device_id_type=MESH)
    pl.semaphore_wait(barrier, 1)
    half = came.shape[0]
    part = half // JOIN_CHUNKS

    def rows(which, c):
        return pl.ds(pl.multiple_of(which * half + c * part, part), part)

    def give(c):
        return pltpu.make_async_remote_copy(
            src_ref=total_ref.at[rows(1 - own, c), :],
            dst_ref=came.at[pl.ds(c * part, part), :],
            send_sem=sems.at[0, c],
            recv_sem=sems.at[1, c],
            device_id={"own": 1 - own},
            device_id_type=MESH,
        )

    for c in range(JOIN_CHUNKS):
        give(c).start()
    for c in range(JOIN_CHUNKS):
        give(c).wait_recv()
        both = total_ref[rows(own, c), :] + came[pl.ds(c * part, part), :]
        out_ref[:, pl.ds(c * part, part)] = both.T.astype(jnp.bfloat16)
    for c in range(JOIN_CHUNKS):
        give(c).wait_send()


def join_halves(total_t):
    width, tok_rows = total_t.shape
    vmem = pl.BlockSpec(memory_space=pltpu.VMEM)
    return pl.pallas_call(
        join_kernel,
        out_shape=jax.ShapeDtypeStruct((tok_rows, width // 2), jnp.bfloat16),
        in_specs=[vmem],
        out_specs=vmem,
        scratch_shapes=[
            pltpu.VMEM((width // 2, tok_rows), jnp.float32),
            pltpu.SemaphoreType.DMA((2, JOIN_CHUNKS)),
        ],
        compiler_params=pltpu.CompilerParams(
            vmem_limit_bytes=48 * MIB, collective_id=1, has_side_effects=True
        ),
        name="join_halves",
    )(total_t)


def per_device(acts, grad_out, weight_blocks, block_rows, block_cols):
    tok_rows, width = acts.shape
    n_data = lax.axis_size("dp")
    data_index = lax.axis_index("dp")
    own_index = lax.axis_index("own")
    local_blocks = weight_blocks.shape[0]
    scale = 1.0 / math.sqrt(tok_rows * n_data)

    w_pairs = (
        weight_blocks.reshape(local_blocks // 2, 2, BLOCK, BLOCK)
        .transpose(0, 2, 1, 3)
        .reshape(local_blocks // 2, BLOCK, LANES)
    )
    n_groups = lax.axis_size("groups")
    side = lax.axis_index("groups") % 2
    w_side = lax.dynamic_slice_in_dim(w_pairs, side * (BLOCK // 2), BLOCK // 2, axis=1)
    w_half = lax.all_gather(w_side, "dp", axis=0, tiled=True)
    acts_t, grad_t = acts.T, grad_out.T
    acts_t, w_side = lax.optimization_barrier((acts_t, w_side))
    a0, g0 = (x.reshape(-1, BLOCK, tok_rows) for x in (acts_t, grad_t))
    a1, g1 = exchange(a0, g0)
    w_half, a1 = lax.optimization_barrier((w_half, a1))
    partners = [[g, g + 1] for g in range(0, n_groups, 2)]
    all_weights = lax.all_gather(w_half, "groups", axis_index_groups=partners)

    owners = n_data // 2
    by_owner_rows = block_rows.reshape(owners, 2, 2, local_blocks)
    by_owner_cols = block_cols.reshape(owners, 2, 2, local_blocks)
    half_rows = by_owner_rows[:, :, own_index]
    half_cols = by_owner_cols[:, :, own_index]

    def from_here(table):
        ours = jnp.roll(table[:, data_index % 2], -(data_index // 2), axis=0)
        return ours.reshape(-1)

    sums = block_grads(
        from_here(half_rows), from_here(half_cols), a0, g0, a1, g1, scale, owners
    )
    later_rows, sums = lax.optimization_barrier((half_rows.reshape(-1), sums))
    grad_blocks = (
        sums.reshape(local_blocks // 2, BLOCK, 2, BLOCK)
        .transpose(0, 2, 1, 3)
        .reshape(local_blocks, BLOCK * BLOCK)
    )
    total_t = input_grad(later_rows, half_cols.reshape(-1), all_weights, grad_t, 8)
    grad_acts = join_halves(total_t)
    return (grad_blocks, grad_acts)


def solution(mesh):
    in_specs = (
        P(("groups", "dp"), None),
        P(("groups", "dp"), None),
        P(("dp", "own"), None),
        P(),
        P(),
    )
    out_specs = (P(("groups", "dp", "own"), None), P(("groups", "dp"), "own"))
    return jax.shard_map(
        per_device, mesh=mesh, in_specs=in_specs, out_specs=out_specs, check_vma=False
    )
```

```python
import functools
import math

import jax
import jax.numpy as jnp
from jax import lax
from jax.experimental import pallas as pl
from jax.experimental.pallas import tpu as pltpu
from jax.sharding import PartitionSpec as P

BLOCK = 64
LANES = 2 * BLOCK
MIB = 1024 * 1024


LEVELS = 32767.0
SMALLEST = 1e-33
CHUNKS = 4
JOIN_CHUNKS = 4
MESH = pl.DeviceIdType.MESH


def exchange_kernel(a0, g0, a1, g1, over_sems, side_sems):
    dp, own = lax.axis_index("dp"), lax.axis_index("own")
    pair = dp + 1 - 2 * lax.rem(dp, 2)
    half = a0.shape[0] // 2
    part = half // CHUNKS

    barrier = pltpu.get_barrier_semaphore()
    pl.semaphore_signal(barrier, inc=1, device_id={"dp": pair}, device_id_type=MESH)
    pl.semaphore_signal(barrier, inc=1, device_id={"own": 1 - own}, device_id_type=MESH)
    pl.semaphore_wait(barrier, 2)

    def over(which, c):
        rows = pl.ds(own * half + c * part, part)
        return pltpu.make_async_remote_copy(
            src_ref=(a0, g0)[which].at[rows],
            dst_ref=(a1, g1)[which].at[rows],
            send_sem=over_sems.at[0, which, c],
            recv_sem=over_sems.at[1, which, c],
            device_id={"dp": pair},
            device_id_type=MESH,
        )

    def side(which, c):
        rows = pl.ds(own * half + c * part, part)
        target = (a1, g1)[which].at[rows]
        return pltpu.make_async_remote_copy(
            src_ref=target,
            dst_ref=target,
            send_sem=side_sems.at[0, which, c],
            recv_sem=side_sems.at[1, which, c],
            device_id={"own": 1 - own},
            device_id_type=MESH,
        )

    order = [(which, c) for c in range(CHUNKS) for which in range(2)]
    for which, c in order:
        over(which, c).start()
    for which, c in order:
        over(which, c).wait_recv()
        side(which, c).start()
    for which, c in order:
        side(which, c).wait_recv()
    for which, c in order:
        over(which, c).wait_send()
        side(which, c).wait_send()


def exchange(a0, g0):
    vmem = pl.BlockSpec(memory_space=pltpu.VMEM)
    return pl.pallas_call(
        exchange_kernel,
        out_shape=(
            jax.ShapeDtypeStruct(a0.shape, a0.dtype),
            jax.ShapeDtypeStruct(g0.shape, g0.dtype),
        ),
        in_specs=[vmem, vmem],
        out_specs=(vmem, vmem),
        scratch_shapes=[
            pltpu.SemaphoreType.DMA((2, 2, CHUNKS)),
            pltpu.SemaphoreType.DMA((2, 2, CHUNKS)),
        ],
        compiler_params=pltpu.CompilerParams(
            vmem_limit_bytes=48 * MIB, collective_id=2, has_side_effects=True
        ),
        name="exchange",
    )(a0, g0)


def block_grad_kernel(
    scale,
    owners,
    rows_ref,
    cols_ref,
    a0,
    g0,
    a1,
    g1,
    out_ref,
    sent,
    sent_unit,
    came,
    came_unit,
    kept,
    word_sems,
    unit_sems,
):
    dp = lax.axis_index("dp")
    n_data = 2 * owners
    each = out_ref.shape[0]
    left_half = lax.broadcasted_iota(jnp.int32, (BLOCK, LANES), 1) < BLOCK

    barrier = pltpu.get_barrier_semaphore()
    for k in range(1, owners):
        pl.semaphore_signal(
            barrier,
            inc=1,
            device_id={"dp": lax.rem(dp + 2 * k, n_data)},
            device_id_type=MESH,
        )
    pl.semaphore_wait(barrier, owners - 1)

    def features(ref, other, at):
        return jnp.concatenate([ref[at], other[at]], axis=1)

    def pair_sum(p):
        b = 2 * p
        lhs = jnp.concatenate([features(a0, a1, rows_ref[b + k]) for k in range(2)], axis=0)
        rhs = jnp.concatenate([features(g0, g1, cols_ref[b + k]) for k in range(2)], axis=0)
        prod = lax.dot_general(
            lhs, rhs, (((1,), (1,)), ((), ())), preferred_element_type=jnp.float32
        )
        return jnp.where(left_half, prod[:BLOCK], prod[BLOCK:]) * scale

    def words(k):
        return pltpu.make_async_remote_copy(
            src_ref=sent.at[k - 1],
            dst_ref=came.at[k - 1],
            send_sem=word_sems.at[0, k - 1],
            recv_sem=word_sems.at[1, k - 1],
            device_id={"dp": lax.rem(dp + 2 * k, n_data)},
            device_id_type=MESH,
        )

    def steps(k):
        return pltpu.make_async_remote_copy(
            src_ref=sent_unit.at[k - 1],
            dst_ref=came_unit.at[k - 1],
            send_sem=unit_sems.at[0, k - 1],
            recv_sem=unit_sems.at[1, k - 1],
            device_id={"dp": lax.rem(dp + 2 * k, n_data)},
            device_id_type=MESH,
        )

    def send_one(k, carry):
        def pack(p, inner):
            total = pair_sum(k * each + p)
            peak = jnp.maximum(jnp.max(jnp.abs(total), axis=0, keepdims=True), SMALLEST)
            levels = jnp.floor(total * (LEVELS / peak) + 0.5).astype(jnp.int32)
            levels = jnp.clip(levels, -32767, 32767)
            sent[k - 1, p] = levels[: BLOCK // 2] * 65536 + levels[BLOCK // 2 :]
            sent_unit[k - 1, pl.ds(p, 1), :] = peak * (1.0 / LEVELS)
            return inner

        lax.fori_loop(0, each, pack, 0, unroll=4)
        words(k).start()
        steps(k).start()
        return carry

    lax.fori_loop(1, owners, send_one, 0)

    def keep(p, carry):
        kept[p] = pair_sum(p)
        return carry

    lax.fori_loop(0, each, keep, 0, unroll=4)

    def wait_one(k, carry):
        words(k).wait_recv()
        steps(k).wait_recv()
        return carry

    lax.fori_loop(1, owners, wait_one, 0)

    def add(p, carry):
        top = kept[p, : BLOCK // 2]
        low = kept[p, BLOCK // 2 :]
        for k in range(owners - 1):
            word = came[k, p]
            unit = came_unit[k, pl.ds(p, 1), :]
            low_levels = lax.shift_right_arithmetic(lax.shift_left(word, 16), 16)
            top_levels = lax.shift_right_arithmetic(word - low_levels, 16)
            top = top + top_levels.astype(jnp.float32) * unit
            low = low + low_levels.astype(jnp.float32) * unit
        out_ref[p] = jnp.concatenate([top, low], axis=0).astype(jnp.bfloat16)
        return carry

    lax.fori_loop(0, each, add, 0, unroll=2)

    def sent_one(k, carry):
        words(k).wait_send()
        steps(k).wait_send()
        return carry

    lax.fori_loop(1, owners, sent_one, 0)


def block_grads(rows, cols, a0, g0, a1, g1, scale, owners):
    each = rows.shape[0] // 2 // owners
    padded = -(-each // 8) * 8
    smem = pl.BlockSpec(memory_space=pltpu.SMEM)
    vmem = pl.BlockSpec(memory_space=pltpu.VMEM)
    return pl.pallas_call(
        functools.partial(block_grad_kernel, scale, owners),
        out_shape=jax.ShapeDtypeStruct((each, BLOCK, LANES), jnp.bfloat16),
        in_specs=[smem, smem, vmem, vmem, vmem, vmem],
        out_specs=vmem,
        scratch_shapes=[
            pltpu.VMEM((owners - 1, each, BLOCK // 2, LANES), jnp.int32),
            pltpu.VMEM((owners - 1, padded, LANES), jnp.float32),
            pltpu.VMEM((owners - 1, each, BLOCK // 2, LANES), jnp.int32),
            pltpu.VMEM((owners - 1, padded, LANES), jnp.float32),
            pltpu.VMEM((each, BLOCK, LANES), jnp.float32),
            pltpu.SemaphoreType.DMA((2, owners - 1)),
            pltpu.SemaphoreType.DMA((2, owners - 1)),
        ],
        compiler_params=pltpu.CompilerParams(
            vmem_limit_bytes=48 * MIB, collective_id=0, has_side_effects=True
        ),
        cost_estimate=pl.CostEstimate(
            flops=100_000_000_000, bytes_accessed=16 * MIB, transcendentals=0
        ),
        name="block_grads",
    )(rows, cols, a0, g0, a1, g1)


def input_grad_kernel(rows_ref, cols_ref, w_ref, g_ref, out_ref):
    pairs = w_ref.shape[1]
    start = pl.program_id(0) * pairs
    lane = lax.broadcasted_iota(jnp.int32, (BLOCK, LANES), 1)
    first = (lane < BLOCK).astype(jnp.float32).astype(jnp.bfloat16)
    second = (lane >= BLOCK).astype(jnp.float32).astype(jnp.bfloat16)

    @pl.when(pl.program_id(0) == 0)
    def _():
        out_ref[...] = jnp.zeros_like(out_ref)

    def span(at):
        return pl.ds(pl.multiple_of(at * BLOCK, BLOCK), BLOCK)

    def one_pair(p, carry):
        b = 2 * (start + p)
        w = jnp.concatenate([w_ref[0, p], w_ref[1, p]], axis=0)
        lhs = jnp.concatenate([w * first, w * second], axis=0)
        rhs = jnp.concatenate([g_ref[span(cols_ref[b + k]), :] for k in range(2)], axis=0)
        prod = jnp.dot(lhs, rhs, preferred_element_type=jnp.float32)
        for k in range(2):
            out_ref[span(rows_ref[b + k]), :] += prod[k * BLOCK : (k + 1) * BLOCK]
        return carry

    lax.fori_loop(0, pairs, one_pair, 0, unroll=13)


def input_grad(rows, cols, weights, g, steps):
    pairs = weights.shape[1]
    return pl.pallas_call(
        input_grad_kernel,
        out_shape=jax.ShapeDtypeStruct(g.shape, jnp.float32),
        grid_spec=pltpu.PrefetchScalarGridSpec(
            num_scalar_prefetch=2,
            grid=(steps,),
            in_specs=[
                pl.BlockSpec(
                    (2, pairs // steps, BLOCK // 2, LANES), lambda i, *_: (0, i, 0, 0)
                ),
                pl.BlockSpec(g.shape, lambda i, *_: (0, 0)),
            ],
            out_specs=pl.BlockSpec(g.shape, lambda i, *_: (0, 0)),
        ),
        compiler_params=pltpu.CompilerParams(vmem_limit_bytes=48 * MIB),
        cost_estimate=pl.CostEstimate(
            flops=pairs * 2 * LANES * LANES * 1024, bytes_accessed=13 * MIB, transcendentals=0
        ),
        name="input_grad",
    )(rows, cols, weights, g)


def join_kernel(total_ref, out_ref, came, sems):
    own = lax.axis_index("own")
    barrier = pltpu.get_barrier_semaphore()
    pl.semaphore_signal(barrier, inc=1, device_id={"own": 1 - own}, device_id_type=MESH)
    pl.semaphore_wait(barrier, 1)
    half = came.shape[0]
    part = half // JOIN_CHUNKS

    def rows(which, c):
        return pl.ds(pl.multiple_of(which * half + c * part, part), part)

    def give(c):
        return pltpu.make_async_remote_copy(
            src_ref=total_ref.at[rows(1 - own, c), :],
            dst_ref=came.at[pl.ds(c * part, part), :],
            send_sem=sems.at[0, c],
            recv_sem=sems.at[1, c],
            device_id={"own": 1 - own},
            device_id_type=MESH,
        )

    for c in range(JOIN_CHUNKS):
        give(c).start()
    for c in range(JOIN_CHUNKS):
        give(c).wait_recv()
        both = total_ref[rows(own, c), :] + came[pl.ds(c * part, part), :]
        out_ref[:, pl.ds(c * part, part)] = both.T.astype(jnp.bfloat16)
    for c in range(JOIN_CHUNKS):
        give(c).wait_send()


def join_halves(total_t):
    width, tok_rows = total_t.shape
    vmem = pl.BlockSpec(memory_space=pltpu.VMEM)
    return pl.pallas_call(
        join_kernel,
        out_shape=jax.ShapeDtypeStruct((tok_rows, width // 2), jnp.bfloat16),
        in_specs=[vmem],
        out_specs=vmem,
        scratch_shapes=[
            pltpu.VMEM((width // 2, tok_rows), jnp.float32),
            pltpu.SemaphoreType.DMA((2, JOIN_CHUNKS)),
        ],
        compiler_params=pltpu.CompilerParams(
            vmem_limit_bytes=48 * MIB, collective_id=1, has_side_effects=True
        ),
        name="join_halves",
    )(total_t)


def per_device(acts, grad_out, weight_blocks, block_rows, block_cols):
    tok_rows, width = acts.shape
    n_data = lax.axis_size("dp")
    data_index = lax.axis_index("dp")
    own_index = lax.axis_index("own")
    local_blocks = weight_blocks.shape[0]
    scale = 1.0 / math.sqrt(tok_rows * n_data)

    w_pairs = (
        weight_blocks.reshape(local_blocks // 2, 2, BLOCK, BLOCK)
        .transpose(0, 2, 1, 3)
        .reshape(local_blocks // 2, BLOCK, LANES)
    )
    n_groups = lax.axis_size("groups")
    side = lax.axis_index("groups") % 2
    w_side = lax.dynamic_slice_in_dim(w_pairs, side * (BLOCK // 2), BLOCK // 2, axis=1)
    w_half = lax.all_gather(w_side, "dp", axis=0, tiled=True)
    acts_t, grad_t = acts.T, grad_out.T
    acts_t, w_side = lax.optimization_barrier((acts_t, w_side))
    a0, g0 = (x.reshape(-1, BLOCK, tok_rows) for x in (acts_t, grad_t))
    a1, g1 = exchange(a0, g0)
    w_half, a1 = lax.optimization_barrier((w_half, a1))
    partners = [[g, g + 1] for g in range(0, n_groups, 2)]
    all_weights = lax.all_gather(w_half, "groups", axis_index_groups=partners)

    owners = n_data // 2
    by_owner_rows = block_rows.reshape(owners, 2, 2, local_blocks)
    by_owner_cols = block_cols.reshape(owners, 2, 2, local_blocks)
    half_rows = by_owner_rows[:, :, own_index]
    half_cols = by_owner_cols[:, :, own_index]

    def from_here(table):
        ours = jnp.roll(table[:, data_index % 2], -(data_index // 2), axis=0)
        return ours.reshape(-1)

    sums = block_grads(
        from_here(half_rows), from_here(half_cols), a0, g0, a1, g1, scale, owners
    )
    later_rows, sums = lax.optimization_barrier((half_rows.reshape(-1), sums))
    grad_blocks = (
        sums.reshape(local_blocks // 2, BLOCK, 2, BLOCK)
        .transpose(0, 2, 1, 3)
        .reshape(local_blocks, BLOCK * BLOCK)
    )
    total_t = input_grad(later_rows, half_cols.reshape(-1), all_weights, grad_t, 8)
    grad_acts = join_halves(total_t)
    return (grad_blocks, grad_acts)


def solution(mesh):
    in_specs = (
        P(("groups", "dp"), None),
        P(("groups", "dp"), None),
        P(("dp", "own"), None),
        P(),
        P(),
    )
    out_specs = (P(("groups", "dp", "own"), None), P(("groups", "dp"), "own"))
    return jax.shard_map(
        per_device, mesh=mesh, in_specs=in_specs, out_specs=out_specs, check_vma=False
    )
```
